512 devices in a mesh: gx: 32 (over z, x_hi), gy: 16 (over y, x_lo, core).
Axes of the slice: x: 4 (x_hi: 2, x_lo: 2; x = x_hi * 2 + x_lo), y: 4, z: 16, core: 2. Of those that a mesh axis runs over, the one named last changes fastest.
Arguments:
- tokens: bfloat16 [512, 16384], P('gy', 'gx'), may hold values from -320 to 320
- gate_weight: bfloat16 [16384, 26624], P('gx', 'gy'), may hold values from -0.046875 to 0.046875
- up_weight: bfloat16 [16384, 26624], P('gx', 'gy'), may hold values from -0.046875 to 0.046875
- down_weight: bfloat16 [26624, 16384], P('gy', 'gx'), may hold values from -0.0390625 to 0.0390625
- sign_bits: int32 [26624], P('gy'), may hold values from 0 to 1
Outputs:
- block_out: bfloat16 [512, 16384], P('gy', 'gx')
The draws below stay inside these ranges and needn't reach their ends.
All inputs are finite; a program needn't handle non-finite values.
Results may differ from the reference program's by a relative error of at most 0.034.
Values may be sent and summed in bfloat16 or wider, within the bound.
No kernel may reach another device: no remote copies, remote signals or barrier semaphores. Data moves between devices by JAX's collectives and lax.ppermute only.
A program may use at most 64 MiB of HBM per device.

```python
import math
import jax
import jax.numpy as jnp
from jax import lax

D = 16384
UNITS = 26624
HAD = 128
TOKENS = 512
N_GX = 32
N_GY = 16


def draw_tokens(key, part):
    key = jax.random.fold_in(key, 11)
    base_key, row_key, col_key = jax.random.split(key, 3)
    row_scale = jnp.exp(jax.random.uniform(row_key, (TOKENS, 1), jnp.float32) * math.log(10.0))
    col_scale = jnp.exp(jax.random.uniform(col_key, (1, D), jnp.float32) * math.log(2.0))
    position = jnp.arange(D, dtype=jnp.float32)[None, :] / (D - 1)
    base = jnp.clip(jax.random.normal(base_key, (TOKENS, D), jnp.float32), -4.0, 4.0)
    ramp = jnp.exp(position * math.log(3.0))
    return (base * row_scale * col_scale * ramp).astype(jnp.bfloat16)


def with_ends(entries, rng, smallest, top_value):
    longest = entries.shape.index(max(entries.shape))
    spots = []
    for shift in (0, 1):
        where = [jax.random.randint(jax.random.fold_in(rng, axis), (), 0, length) for axis, length in enumerate(entries.shape)]
        where[longest] = (where[longest] + shift) % entries.shape[longest]
        spots.append(tuple(where))
    return entries.at[spots[0]].set(smallest).at[spots[1]].set(top_value)


def level_of(rng, shape, cuts, least, top_value):
    gain, own = 1.0, jax.random.fold_in(rng, 6)
    for dim, blocks in cuts:
        heights = jnp.exp(jax.random.uniform(jax.random.fold_in(own, dim), (blocks,), jnp.float32, least / len(cuts), top_value / len(cuts)))
        gain = gain * jnp.repeat(heights, shape[dim] // blocks).reshape([-1 if axis == dim else 1 for axis in range(len(shape))])
    return gain


def centred(rng, shape, scale, most, shards=(), kind=jnp.bfloat16):
    loudness = level_of(rng, shape, shards, -0.22, 0.18) if shards else 1.0
    drawn = jax.random.normal(rng, shape, jnp.float32) * scale * loudness
    return jnp.minimum(jnp.maximum(drawn, -most), most).astype(kind)


def setup_inputs(seed: int = 0) -> dict:
    key_list = jax.random.split(jax.random.key(seed), 6)
    tokens = draw_tokens(jax.random.fold_in(key_list[5], 71), 0)
    gate_weight = centred(key_list[1], (D, UNITS), D ** -0.5, 0.046875, ((0, 32), (1, 16)))
    up_weight = centred(key_list[2], (D, UNITS), D ** -0.5, 0.046875, ((0, 32), (1, 16)))
    down_weight = centred(key_list[3], (UNITS, D), UNITS ** -0.5, 0.0390625, ((0, 16), (1, 32)))
    sign_bits = with_ends(jax.random.randint(key_list[4], (UNITS,), 0, 2), jax.random.fold_in(key_list[4], 1), 0, 1).astype(jnp.int32)
    return {"tokens": tokens, "gate_weight": gate_weight, "up_weight": up_weight, "down_weight": down_weight, "sign_bits": sign_bits}


epsilon = 1e-05

def hadamard():
    row_index = jnp.arange(HAD, dtype=jnp.int32)[:, None]
    col_index = jnp.arange(HAD, dtype=jnp.int32)[None, :]
    parity = jnp.zeros((HAD, HAD), jnp.int32)
    for bit in range(HAD.bit_length() - 1):
        parity = parity + jnp.bitwise_and(jnp.right_shift(row_index, bit), 1) * jnp.bitwise_and(jnp.right_shift(col_index, bit), 1)
    return jnp.where(parity % 2 == 0, 1.0, -1.0).astype(jnp.bfloat16)

def reference(tokens, gate_weight, up_weight, down_weight, sign_bits):
    values = tokens.astype(jnp.float32)
    inverse = lax.rsqrt(lax.optimization_barrier(jnp.mean(values * values, axis=1)) + epsilon)
    normed = (values * inverse[:, None]).astype(jnp.bfloat16)
    width_shard = D // N_GX

    def first_sum(step, carry):
        start = (step * width_shard).astype(jnp.int32)
        rows = lax.dynamic_slice_in_dim(normed, start, width_shard, 1)
        gate_part = jnp.dot(rows, lax.dynamic_slice_in_dim(gate_weight, start, width_shard, 0), preferred_element_type=jnp.float32)
        up_part = jnp.dot(rows, lax.dynamic_slice_in_dim(up_weight, start, width_shard, 0), preferred_element_type=jnp.float32)
        gate_part = lax.optimization_barrier(gate_part.astype(jnp.bfloat16)).astype(jnp.float32)
        up_part = lax.optimization_barrier(up_part.astype(jnp.bfloat16)).astype(jnp.float32)
        return (carry[0] + gate_part, carry[1] + up_part)
    empty = jnp.zeros((TOKENS, UNITS), jnp.float32)
    gate_sum, up_sum = lax.fori_loop(0, N_GX, first_sum, (empty, empty))
    hidden = (jax.nn.silu(gate_sum) * up_sum).astype(jnp.bfloat16)
    signs = (2 * sign_bits - 1).astype(jnp.bfloat16)
    signed = hidden * signs[None, :]
    blocks = signed.reshape(TOKENS * (UNITS // HAD), HAD)
    rotated = (jnp.dot(blocks, hadamard(), preferred_element_type=jnp.float32) * HAD ** (-0.5)).reshape(TOKENS, UNITS).astype(jnp.bfloat16)
    unit_shard = UNITS // N_GY

    def second_sum(step, total):
        start = (step * unit_shard).astype(jnp.int32)
        part = jnp.dot(lax.dynamic_slice_in_dim(rotated, start, unit_shard, 1), lax.dynamic_slice_in_dim(down_weight, start, unit_shard, 0), preferred_element_type=jnp.float32)
        return total + lax.optimization_barrier(part.astype(jnp.bfloat16)).astype(jnp.float32)
    total = lax.fori_loop(0, N_GY, second_sum, jnp.zeros((TOKENS, D), jnp.float32))
    return total.astype(jnp.bfloat16)
```

```python
import jax
import jax.numpy as jnp
import numpy as np
from jax import lax
from jax.experimental import pallas as pl
from jax.experimental.pallas import tpu as pltpu
from jax.sharding import Mesh, PartitionSpec as P

D = 16384
HAD = 128
UNITS = 1664
LANES = 128
EPSILON = 1e-05

AXES = ("zh", "zl", "xh", "y", "xl", "c")
SIZES = (4, 4, 2, 4, 2, 2)
GX = ("zh", "zl", "xh")
GY = ("y", "xl", "c")
Z = ("zh", "zl")
f32, bf16 = jnp.float32, jnp.bfloat16


def along_z(x, d):
    return lax.ppermute(x, Z, [(i, (i + d) % 16) for i in range(16)])


def across_x(x):
    return lax.ppermute(x, "xh", [(0, 1), (1, 0)])


def dot(a, b):
    return jnp.dot(a, b, preferred_element_type=f32)


def hadamard():
    i = np.arange(HAD)
    both = i[:, None] & i[None, :]
    parity = np.zeros_like(both)
    for bit in range(7):
        parity ^= (both >> bit) & 1
    return jnp.asarray(1.0 - 2.0 * parity, bf16)


def finish(own, a, b, c, signs, had, out):
    def total(lo, hi):
        return (own[:, lo:hi].astype(f32) + a[:, lo:hi].astype(f32)
                + b[:, lo:hi].astype(f32) + c[:, lo:hi].astype(f32))

    squares = jnp.sum(total(2 * UNITS, 2 * UNITS + LANES), axis=1, keepdims=True)
    inverse = lax.rsqrt(squares / D + EPSILON)
    for k in range(UNITS // HAD):
        lo = k * HAD
        gate = total(lo, lo + HAD) * inverse
        up = total(UNITS + lo, UNITS + lo + HAD) * inverse
        hidden = (gate / (1.0 + jnp.exp(-gate)) * up).astype(bf16)
        signed = hidden * signs[:, lo:lo + HAD]
        out[:, lo:lo + HAD] = (dot(signed, had[...]) * HAD ** (-0.5)).astype(bf16)


def local(tokens, gate_weight, up_weight, down_weight, sign_bits):
    zh, zl, xh = lax.axis_index("zh"), lax.axis_index("zl"), lax.axis_index("xh")

    sent = jnp.concatenate([tokens] * 8, axis=0)
    some = lax.all_to_all(sent, ("y", "xl"), 0, 0, tiled=True)
    gathered = lax.all_gather(some, "c", axis=0, tiled=True)

    rows = gathered.reshape(2, 4, 64, 512)

    def gate_of(x):
        t = lax.dynamic_index_in_dim(rows, x, 0, keepdims=False).reshape(256, 512)
        return dot(t, gate_weight)

    def up_of(d):
        t = lax.dynamic_index_in_dim(rows, (zl + d) % 4, 1, keepdims=False).reshape(128, 512)
        v = t.astype(f32)
        v = v * v
        squares = v[:, :128] + v[:, 128:256] + v[:, 256:384] + v[:, 384:]
        return jnp.concatenate([dot(t, up_weight).astype(bf16), squares.astype(bf16)], axis=1)

    gate_in = across_x(gate_of(1 - xh).astype(bf16))
    up2 = up_of(2).reshape(2, 64, UNITS + LANES)
    up_a = along_z(up2[:, :32], 2)
    up_b = along_z(up2[:, 32:], -2)
    up_c = along_z(up_of(1), 1)
    up_d = along_z(up_of(3), -1)
    up_own = up_of(0).astype(f32).reshape(2, 64, UNITS + LANES)
    gate_own = gate_of(xh)

    gate = (gate_own + gate_in.astype(f32)).astype(bf16).reshape(4, 64, UNITS)

    def gate_class(d):
        return lax.dynamic_index_in_dim(gate, (zl + d) % 4, 0, keepdims=False)

    gate2 = gate_class(2)
    gate_a = along_z(gate2[:32], 2)
    gate_b = along_z(gate2[32:], -2)
    gate_c = along_z(gate_class(1), 1)
    gate_d = along_z(gate_class(3), -1)
    up = up_own + up_c.reshape(up_own.shape).astype(f32) + up_d.reshape(up_own.shape).astype(f32)
    up = up + jnp.concatenate([up_a, up_b], axis=1).astype(f32)
    up_in = across_x(lax.dynamic_index_in_dim(up, 1 - xh, 0, keepdims=False).astype(bf16))
    up = lax.dynamic_index_in_dim(up, xh, 0, keepdims=False) + up_in.astype(f32)
    gate = gate_class(0).astype(f32) + gate_c.astype(f32) + gate_d.astype(f32)
    gate = gate + jnp.concatenate([gate_a, gate_b], axis=0).astype(f32)

    both = jnp.concatenate([gate.astype(bf16), up.astype(bf16)], axis=1).reshape(2, 4, 8, 2 * UNITS + LANES)

    def both_class(d):
        return lax.dynamic_index_in_dim(both, (zh + d) % 4, 1, keepdims=False).reshape(16, 2 * UNITS + LANES)

    far_c = along_z(both_class(2), 8)
    far_a = along_z(both_class(1), 4)
    far_b = along_z(both_class(3), -4)

    signs = (2 * sign_bits - 1).astype(bf16).reshape(1, UNITS)
    rotated = pl.pallas_call(
        finish,
        out_shape=jax.ShapeDtypeStruct((16, UNITS), bf16),
    )(both_class(0), far_a, far_b, far_c, signs, hadamard())

    from_p2 = along_z(rotated, 8)
    from_m1 = along_z(rotated, 4)
    from_p1 = along_z(rotated, -4)
    far = jnp.concatenate([rotated, from_p1, from_p2, from_m1], axis=0)
    near = lax.all_gather(far, "xh", axis=0, tiled=True)
    n2a = along_z(near[:64], 2)
    n2b = along_z(near[64:], -2)
    n3 = along_z(near, 1)
    n1 = along_z(near, -1)
    pieces = [dot(v, down_weight).astype(bf16) for v in (near, n1, n2a, n2b, n3)]
    out = jnp.concatenate(pieces, axis=0)

    r = lax.broadcasted_iota(jnp.int32, (512, 512), 1)
    d, x, j, half, k = r // 128, r // 64 % 2, r // 16 % 4, r // 8 % 2, r % 8
    shift = jnp.where(d == 0, 0, jnp.where(d == 1, 1, jnp.where(d == 3, -1, jnp.where(x == 0, -2, 2))))
    sender = (zh * 4 + zl + shift + 16) % 16
    place = (((x * 4 + sender % 4) * 2 + half) * 4 + (sender // 4 + j) % 4) * 8 + k
    order = (place == lax.broadcasted_iota(jnp.int32, (512, 512), 0)).astype(bf16)
    out = dot(order, out).astype(bf16)

    parts = lax.all_to_all(out.reshape(16, 32, 512), ("c", "y", "xl"), 0, 0, tiled=True)
    return jnp.sum(parts.astype(f32), axis=0).astype(bf16)


def solution(mesh):
    fine = Mesh(mesh.devices.reshape(SIZES), AXES)
    return jax.shard_map(
        local,
        mesh=fine,
        in_specs=(P(GY, GX), P(GX, GY), P(GX, GY), P(GY, GX), P(GY)),
        out_specs=P(GY, GX),
        check_vma=False,
    )
```

```python
import jax
import jax.numpy as jnp
import numpy as np
from jax import lax
from jax.experimental import pallas as pl
from jax.experimental.pallas import tpu as pltpu
from jax.sharding import Mesh, PartitionSpec as P

D = 16384
HAD = 128
UNITS = 1664
LANES = 128
EPSILON = 1e-05

AXES = ("zh", "zl", "xh", "y", "xl", "c")
SIZES = (4, 4, 2, 4, 2, 2)
GX = ("zh", "zl", "xh")
GY = ("y", "xl", "c")
Z = ("zh", "zl")
f32, bf16 = jnp.float32, jnp.bfloat16


def along_z(x, d):
    return lax.ppermute(x, Z, [(i, (i + d) % 16) for i in range(16)])


def two_along_z(x):
    return lax.ppermute(x, Z, [(i, (i + (-2 if i % 2 else 2)) % 16) for i in range(16)])


def across_x(x):
    return lax.ppermute(x, "xh", [(0, 1), (1, 0)])


def dot(a, b):
    return jnp.dot(a, b, preferred_element_type=f32)


def hadamard():
    i = np.arange(HAD)
    both = i[:, None] & i[None, :]
    parity = np.zeros_like(both)
    for bit in range(7):
        parity ^= (both >> bit) & 1
    return jnp.asarray(1.0 - 2.0 * parity, bf16)


def finish(own, a, b, c, signs, had, out):
    def total(lo, hi):
        return (own[:, lo:hi].astype(f32) + a[:, lo:hi].astype(f32)
                + b[:, lo:hi].astype(f32) + c[:, lo:hi].astype(f32))

    squares = jnp.sum(total(2 * UNITS, 2 * UNITS + LANES), axis=1, keepdims=True)
    inverse = lax.rsqrt(squares / D + EPSILON)
    for k in range(UNITS // HAD):
        lo = k * HAD
        gate = total(lo, lo + HAD) * inverse
        up = total(UNITS + lo, UNITS + lo + HAD) * inverse
        hidden = (gate / (1.0 + jnp.exp(-gate)) * up).astype(bf16)
        signed = hidden * signs[:, lo:lo + HAD]
        out[:, lo:lo + HAD] = (dot(signed, had[...]) * HAD ** (-0.5)).astype(bf16)


def local(tokens, gate_weight, up_weight, down_weight, sign_bits):
    zh, zl, xh = lax.axis_index("zh"), lax.axis_index("zl"), lax.axis_index("xh")

    sent = jnp.broadcast_to(tokens[None], (8, 32, 512))
    some = lax.all_to_all(sent, ("y", "xl"), 0, 0, tiled=True).reshape(256, 512)
    gathered = lax.all_gather(some, "c", axis=0, tiled=True)

    rows = gathered.reshape(4, 2, 64, 512)

    def gate_of(x):
        t = lax.dynamic_index_in_dim(rows, x, 1, keepdims=False).reshape(256, 512)
        return dot(t, gate_weight)

    def up_of(d, after=None):
        t = lax.dynamic_index_in_dim(rows, (zl + d) % 4, 0, keepdims=False).reshape(128, 512)
        if after is not None:
            t, _ = lax.optimization_barrier((t, after))
        v = t.astype(f32)
        v = v * v
        squares = v[:, :128] + v[:, 128:256] + v[:, 256:384] + v[:, 384:]
        return jnp.concatenate([dot(t, up_weight).astype(bf16), squares.astype(bf16)], axis=1)

    gate_out = gate_of(1 - xh).astype(bf16)
    gate_in = across_x(gate_out)
    up1 = up_of(1, gate_out)
    up_c = along_z(up1, 1)
    up3 = up_of(3, up1)
    up_d = along_z(up3, -1)
    up2 = up_of(2, up3)
    up_a = two_along_z(up2)
    up_own = up_of(0, up2).astype(f32)
    gate_own = gate_of(xh)

    gate = (gate_own + gate_in.astype(f32)).astype(bf16).reshape(4, 64, UNITS)

    def gate_class(d):
        return lax.dynamic_index_in_dim(gate, (zl + d) % 4, 0, keepdims=False)

    gate_c = along_z(gate_class(1), 1)
    gate_d = along_z(gate_class(3), -1)
    gate_a = two_along_z(gate_class(2))
    up = (up_own + up_c.astype(f32) + up_d.astype(f32) + up_a.astype(f32)).reshape(2, 64, UNITS + LANES)
    up_in = across_x(lax.dynamic_index_in_dim(up, 1 - xh, 0, keepdims=False).astype(bf16))
    up = lax.dynamic_index_in_dim(up, xh, 0, keepdims=False) + up_in.astype(f32)
    gate = gate_class(0).astype(f32) + gate_c.astype(f32) + gate_d.astype(f32) + gate_a.astype(f32)

    both = jnp.concatenate([gate.astype(bf16), up.astype(bf16)], axis=1).reshape(2, 4, 8, 2 * UNITS + LANES)

    def both_class(d):
        return lax.dynamic_index_in_dim(both, (zh + d) % 4, 1, keepdims=False).reshape(16, 2 * UNITS + LANES)

    far_a = along_z(both_class(1), 4)
    far_b = along_z(both_class(3), -4)
    far_c = along_z(both_class(2), 8)

    signs = (2 * sign_bits - 1).astype(bf16).reshape(1, UNITS)
    rotated = pl.pallas_call(
        finish,
        out_shape=jax.ShapeDtypeStruct((16, UNITS), bf16),
    )(both_class(0), far_a, far_b, far_c, signs, hadamard())

    far = lax.all_gather(rotated, "zh", axis=0, tiled=True)
    near = lax.all_gather(far, "xh", axis=0, tiled=True)
    n3 = along_z(near, 1)
    n1 = along_z(near, -1)
    n2 = two_along_z(near)
    pieces = [dot(v, down_weight).astype(bf16) for v in (near, n1, n2, n3)]
    out = jnp.concatenate(pieces, axis=0)

    r = lax.broadcasted_iota(jnp.int32, (512, 512), 1)
    d, x, far_z, half, k = r // 128, r // 64 % 2, r // 16 % 4, r // 8 % 2, r % 8
    place = ((((zl + d) % 4 * 2 + x) * 2 + half) * 4 + far_z) * 8 + k
    order = (place == lax.broadcasted_iota(jnp.int32, (512, 512), 0)).astype(bf16)
    out = dot(order, out).astype(bf16)

    parts = lax.all_to_all(out.reshape(16, 32, 512), ("c", "y", "xl"), 0, 0, tiled=True)
    return jnp.sum(parts.astype(f32), axis=0).astype(bf16)


def solution(mesh):
    fine = Mesh(mesh.devices.reshape(SIZES), AXES)
    return jax.shard_map(
        local,
        mesh=fine,
        in_specs=(P(GY, GX), P(GX, GY), P(GX, GY), P(GY, GX), P(GY)),
        out_specs=P(GY, GX),
        check_vma=False,
    )
```

```python
import jax
import jax.numpy as jnp
from jax import lax
from jax.experimental import pallas as pl
from jax.experimental.pallas import tpu as pltpu
from jax.sharding import Mesh, PartitionSpec as P

D = 16384
HAD = 128
UNITS = 1664
LANES = 128
EPSILON = 1e-05

AXES = ("zh", "zl", "xh", "y", "xl", "c")
SIZES = (4, 4, 2, 4, 2, 2)
GX = ("zh", "zl", "xh")
GY = ("y", "xl", "c")
Z = ("zh", "zl")
f32, bf16 = jnp.float32, jnp.bfloat16


def along_z(x, d):
    return lax.ppermute(x, Z, [(i, (i + d) % 16) for i in range(16)])


def two_along_z(x):
    return lax.ppermute(x, Z, [(i, (i + (-2 if i % 2 else 2)) % 16) for i in range(16)])


def across_x(x):
    return lax.ppermute(x, "xh", [(0, 1), (1, 0)])


def dot(a, b):
    return jnp.dot(a, b, preferred_element_type=f32)


def finish(own, a, b, c, sign_bits, out):
    def total(lo, hi):
        return (own[:, lo:hi].astype(f32) + a[:, lo:hi].astype(f32)
                + b[:, lo:hi].astype(f32) + c[:, lo:hi].astype(f32))

    both = lax.broadcasted_iota(jnp.int32, (HAD, HAD), 0) & lax.broadcasted_iota(jnp.int32, (HAD, HAD), 1)
    both = both ^ (both >> 4)
    both = both ^ (both >> 2)
    both = both ^ (both >> 1)
    had = (1 - 2 * (both & 1)).astype(f32).astype(bf16)
    squares = jnp.sum(total(UNITS, UNITS + LANES), axis=1, keepdims=True)
    inverse = lax.rsqrt(squares / D + EPSILON)
    for k in range(UNITS // HAD):
        lo = k * HAD
        gate = total(lo, lo + HAD) * inverse
        up = total(UNITS + LANES + lo, UNITS + LANES + lo + HAD) * inverse
        hidden = (gate / (1.0 + jnp.exp(-gate)) * up).astype(bf16)
        signed = (hidden.astype(f32) * (2 * sign_bits[:, lo:lo + HAD] - 1).astype(f32)).astype(bf16)
        out[:, lo:lo + HAD] = (dot(signed, had) * HAD ** (-0.5)).astype(bf16)


def local(tokens, gate_weight, up_weight, down_weight, sign_bits):
    zh, zl, xh = lax.axis_index("zh"), lax.axis_index("zl"), lax.axis_index("xh")

    def pick(x, i, axis):
        return lax.dynamic_index_in_dim(x, i, axis, keepdims=False)

    sent = jnp.broadcast_to(tokens[None], (8, 32, 512))
    some = lax.all_to_all(sent, ("y", "xl"), 0, 0, tiled=True).reshape(256, 512)
    gathered = lax.all_gather(some, "c", axis=0, tiled=True)

    rows = gathered.reshape(2, 8, 4, 8, 512)

    def gate_of(x, after):
        t = pick(rows, x, 0).reshape(256, 512)
        t, _ = lax.optimization_barrier((t, after))
        v = t.astype(f32)
        v = v * v
        squares = v[:, :128] + v[:, 128:256] + v[:, 256:384] + v[:, 384:]
        return jnp.concatenate([dot(t, gate_weight), squares], axis=1)

    def up_of(d, after):
        t = pick(rows, (zl + d) & 3, 2).reshape(128, 512)
        t, _ = lax.optimization_barrier((t, after))
        return dot(t, up_weight).astype(bf16)

    up1 = up_of(1, tokens)
    up_c = along_z(up1, 1)
    up3 = up_of(3, up1)
    up_d = along_z(up3, -1)
    gate_out = gate_of(1 - xh, up3).astype(bf16)
    gate_in = across_x(gate_out)
    up2 = up_of(2, gate_out)
    up_a = two_along_z(up2)
    up_own = up_of(0, up2).astype(f32)
    gate_own = gate_of(xh, up2)

    gate = (gate_own + gate_in.astype(f32)).astype(bf16).reshape(8, 4, 8, UNITS + LANES)

    def gate_class(d):
        return pick(gate, (zl + d) & 3, 1).reshape(64, UNITS + LANES)

    gate_c = along_z(gate_class(1), 1)
    gate_d = along_z(gate_class(3), -1)
    gate_a = two_along_z(gate_class(2))
    up = (up_own + up_c.astype(f32) + up_d.astype(f32) + up_a.astype(f32)).reshape(2, 64, UNITS)
    up_in = across_x(pick(up, 1 - xh, 0).astype(bf16))
    up = pick(up, xh, 0) + up_in.astype(f32)
    gate = gate_class(0).astype(f32) + gate_c.astype(f32) + gate_d.astype(f32) + gate_a.astype(f32)

    both = jnp.concatenate([gate.astype(bf16), up.astype(bf16)], axis=1).reshape(4, 16, 2 * UNITS + LANES)
    far_a = along_z(pick(both, (zh + 1) & 3, 0), 4)
    far_b = along_z(pick(both, (zh + 3) & 3, 0), -4)
    far_c = along_z(pick(both, (zh + 2) & 3, 0), 8)

    rotated = pl.pallas_call(
        finish,
        out_shape=jax.ShapeDtypeStruct((16, UNITS), bf16),
        compiler_params=pltpu.CompilerParams(vmem_limit_bytes=4 * 1024 * 1024),
    )(pick(both, zh, 0), far_a, far_b, far_c, sign_bits.reshape(1, UNITS))

    mine = lax.all_gather(rotated, "zh", axis=0, tiled=True)
    theirs = across_x(mine)

    def from_near(v):
        return v, along_z(v, -1), two_along_z(v), along_z(v, 1)

    def out_of(v):
        return dot(v, down_weight).astype(bf16).reshape(8, 8, 512)

    own = [out_of(v) for v in from_near(mine)]
    other = [out_of(v) for v in from_near(theirs)]
    first = jnp.concatenate([jnp.where(xh == 0, p, q) for p, q in zip(own, other)], axis=1)
    second = jnp.concatenate([jnp.where(xh == 0, q, p) for p, q in zip(own, other)], axis=1)
    parts = lax.all_to_all(jnp.concatenate([first, second], axis=0), ("c", "y", "xl"), 0, 0, tiled=True)
    out = jnp.sum(parts.astype(f32), axis=0).astype(bf16)

    out = jnp.concatenate([out, out], axis=0)
    return lax.dynamic_slice_in_dim(out, ((4 - zl) & 3) * 8, 32, 0)


def solution(mesh):
    fine = Mesh(mesh.devices.reshape(SIZES), AXES)
    return jax.shard_map(
        local,
        mesh=fine,
        in_specs=(P(GY, GX), P(GX, GY), P(GX, GY), P(GY, GX), P(GY)),
        out_specs=P(GY, GX),
        check_vma=False,
    )
```

```python
import jax
import jax.numpy as jnp
from jax import lax
from jax.experimental import pallas as pl
from jax.experimental.pallas import tpu as pltpu
from jax.sharding import Mesh, PartitionSpec as P

D = 16384
HAD = 128
UNITS = 1664
LANES = 128
EPSILON = 1e-05

AXES = ("zh", "zl", "xh", "y", "xl", "c")
SIZES = (4, 4, 2, 4, 2, 2)
GX = ("zh", "zl", "xh")
GY = ("y", "xl", "c")
Z = ("zh", "zl")
f32, bf16 = jnp.float32, jnp.bfloat16


def along_z(x, d):
    return lax.ppermute(x, Z, [(i, (i + d) % 16) for i in range(16)])


def two_along_z(x):
    return lax.ppermute(x, Z, [(i, (i + (-2 if i % 2 else 2)) % 16) for i in range(16)])


def across_x(x):
    return lax.ppermute(x, "xh", [(0, 1), (1, 0)])


def dot(a, b):
    return jnp.dot(a, b, preferred_element_type=f32)


def finish(own, a, b, c, sign_bits, out):
    def total(lo, hi):
        return (own[:, lo:hi].astype(f32) + a[:, lo:hi].astype(f32)
                + b[:, lo:hi].astype(f32) + c[:, lo:hi].astype(f32))

    both = lax.broadcasted_iota(jnp.int32, (HAD, HAD), 0) & lax.broadcasted_iota(jnp.int32, (HAD, HAD), 1)
    both = both ^ (both >> 4)
    both = both ^ (both >> 2)
    both = both ^ (both >> 1)
    had = (1 - 2 * (both & 1)).astype(f32).astype(bf16)
    squares = jnp.sum(total(UNITS, UNITS + LANES), axis=1, keepdims=True)
    inverse = lax.rsqrt(squares / D + EPSILON)
    for k in range(UNITS // HAD):
        lo = k * HAD
        gate = total(lo, lo + HAD) * inverse
        up = total(UNITS + LANES + lo, UNITS + LANES + lo + HAD) * inverse
        hidden = (gate / (1.0 + jnp.exp(-gate)) * up).astype(bf16)
        signed = (hidden.astype(f32) * (2 * sign_bits[:, lo:lo + HAD] - 1).astype(f32)).astype(bf16)
        out[:, lo:lo + HAD] = (dot(signed, had) * HAD ** (-0.5)).astype(bf16)


def local(tokens, gate_weight, up_weight, down_weight, sign_bits):
    zh, zl, xh = lax.axis_index("zh"), lax.axis_index("zl"), lax.axis_index("xh")

    def pick(x, i, axis):
        return lax.dynamic_index_in_dim(x, i, axis, keepdims=False)

    sent = jnp.broadcast_to(tokens[None], (8, 32, 512))
    some = lax.all_to_all(sent, ("y", "xl"), 0, 0, tiled=True).reshape(256, 512)
    gathered = lax.all_gather(some, "c", axis=0, tiled=True)

    rows = gathered.reshape(2, 8, 4, 8, 512)

    def gate_of(x, after):
        t = pick(rows, x, 0).reshape(256, 512)
        t, _ = lax.optimization_barrier((t, after))
        v = t.astype(f32)
        v = v * v
        squares = v[:, :128] + v[:, 128:256] + v[:, 256:384] + v[:, 384:]
        return jnp.concatenate([dot(t, gate_weight), squares], axis=1)

    def up_of(d, after):
        t = pick(rows, (zl + d) & 3, 2).reshape(128, 512)
        t, _ = lax.optimization_barrier((t, after))
        return dot(t, up_weight).astype(bf16)

    up1 = up_of(1, tokens)
    up_c = along_z(up1, 1)
    gate_out = gate_of(1 - xh, up1).astype(bf16)
    gate_in = across_x(gate_out)
    up3 = up_of(3, gate_out)
    up_d = along_z(up3, -1)
    up2 = up_of(2, up3)
    up_a = two_along_z(up2)
    up_own = up_of(0, up2).astype(f32)
    gate_own = gate_of(xh, up2)

    gate = (gate_own + gate_in.astype(f32)).astype(bf16).reshape(8, 4, 8, UNITS + LANES)

    def gate_class(d):
        return pick(gate, (zl + d) & 3, 1).reshape(64, UNITS + LANES)

    gate_c = along_z(gate_class(1), 1)
    gate_d = along_z(gate_class(3), -1)
    gate_a = two_along_z(gate_class(2))
    up = (up_own + up_c.astype(f32) + up_d.astype(f32) + up_a.astype(f32)).reshape(2, 64, UNITS)
    up_in = across_x(pick(up, 1 - xh, 0).astype(bf16))
    up = pick(up, xh, 0) + up_in.astype(f32)
    gate = gate_class(0).astype(f32) + gate_c.astype(f32) + gate_d.astype(f32) + gate_a.astype(f32)

    both = jnp.concatenate([gate.astype(bf16), up.astype(bf16)], axis=1).reshape(4, 16, 2 * UNITS + LANES)
    far_a = along_z(pick(both, (zh + 1) & 3, 0), 4)
    far_b = along_z(pick(both, (zh + 3) & 3, 0), -4)
    far_c = along_z(pick(both, (zh + 2) & 3, 0), 8)

    rotated = pl.pallas_call(
        finish,
        out_shape=jax.ShapeDtypeStruct((16, UNITS), bf16),
        compiler_params=pltpu.CompilerParams(vmem_limit_bytes=4 * 1024 * 1024),
    )(pick(both, zh, 0), far_a, far_b, far_c, sign_bits.reshape(1, UNITS))

    far = lax.all_gather(rotated, "zh", axis=0, tiled=True)
    near = lax.all_gather(far, "xh", axis=0, tiled=True)
    n3 = along_z(near, 1)
    n1 = along_z(near, -1)
    n2 = jnp.concatenate([along_z(n1[:64], -1), along_z(n3[64:], 1)], axis=0)

    def out_of(group):
        pieces = [dot(v, down_weight).astype(bf16).reshape(16, 8, 512) for v in group]
        parts = lax.all_to_all(jnp.concatenate(pieces, axis=1), ("c", "y", "xl"), 0, 0, tiled=True)
        return jnp.sum(parts.astype(f32), axis=0).astype(bf16)

    out = jnp.concatenate([out_of(group) for group in ((near, n1, n2, n3),)], axis=0)
    out = jnp.concatenate([out, out], axis=0)
    return lax.dynamic_slice_in_dim(out, ((4 - zl) & 3) * 8, 32, 0)


def solution(mesh):
    fine = Mesh(mesh.devices.reshape(SIZES), AXES)
    return jax.shard_map(
        local,
        mesh=fine,
        in_specs=(P(GY, GX), P(GX, GY), P(GX, GY), P(GY, GX), P(GY)),
        out_specs=P(GY, GX),
        check_vma=False,
    )
```

```python
import jax
import jax.numpy as jnp
from jax import lax
from jax.experimental import pallas as pl
from jax.experimental.pallas import tpu as pltpu
from jax.sharding import Mesh, PartitionSpec as P

D = 16384
HAD = 128
UNITS = 1664
LANES = 128
EPSILON = 1e-05

AXES = ("zh", "zl", "xh", "y", "xl", "c")
SIZES = (4, 4, 2, 4, 2, 2)
GX = ("zh", "zl", "xh")
GY = ("y", "xl", "c")
Z = ("zh", "zl")
f32, bf16 = jnp.float32, jnp.bfloat16


def along_z(x, d):
    return lax.ppermute(x, Z, [(i, (i + d) % 16) for i in range(16)])


def two_along_z(x):
    return lax.ppermute(x, Z, [(i, (i + (-2 if i % 2 else 2)) % 16) for i in range(16)])


def across_x(x):
    return lax.ppermute(x, "xh", [(0, 1), (1, 0)])


def dot(a, b):
    return jnp.dot(a, b, preferred_element_type=f32)


def finish(own, a, b, c, sign_bits, out):
    def total(lo, hi):
        return (own[:, lo:hi].astype(f32) + a[:, lo:hi].astype(f32)
                + b[:, lo:hi].astype(f32) + c[:, lo:hi].astype(f32))

    both = lax.broadcasted_iota(jnp.int32, (HAD, HAD), 0) & lax.broadcasted_iota(jnp.int32, (HAD, HAD), 1)
    both = both ^ (both >> 4)
    both = both ^ (both >> 2)
    both = both ^ (both >> 1)
    had = (1 - 2 * (both & 1)).astype(f32).astype(bf16)
    squares = jnp.sum(total(UNITS, UNITS + LANES), axis=1, keepdims=True)
    inverse = lax.rsqrt(squares / D + EPSILON)
    for k in range(UNITS // HAD):
        lo = k * HAD
        gate = total(lo, lo + HAD) * inverse
        up = total(UNITS + LANES + lo, UNITS + LANES + lo + HAD) * inverse
        hidden = (gate / (1.0 + jnp.exp(-gate)) * up).astype(bf16)
        signed = (hidden.astype(f32) * (2 * sign_bits[:, lo:lo + HAD] - 1).astype(f32)).astype(bf16)
        out[:, lo:lo + HAD] = (dot(signed, had) * HAD ** (-0.5)).astype(bf16)


def local(tokens, gate_weight, up_weight, down_weight, sign_bits):
    zh, zl, xh = lax.axis_index("zh"), lax.axis_index("zl"), lax.axis_index("xh")

    def pick(x, i, axis):
        return lax.dynamic_index_in_dim(x, i, axis, keepdims=False)

    sent = jnp.broadcast_to(tokens[None], (8, 32, 512))
    some = lax.all_to_all(sent, ("y", "xl"), 0, 0, tiled=True).reshape(256, 512)
    gathered = lax.all_gather(some, "c", axis=0, tiled=True)

    rows = gathered.reshape(2, 8, 4, 8, 512)

    def gate_of(x, after):
        t = pick(rows, x, 0).reshape(256, 512)
        t, _ = lax.optimization_barrier((t, after))
        v = t.astype(f32)
        v = v * v
        squares = v[:, :128] + v[:, 128:256] + v[:, 256:384] + v[:, 384:]
        return jnp.concatenate([dot(t, gate_weight), squares], axis=1)

    def up_of(d, after):
        t = pick(rows, (zl + d) & 3, 2).reshape(128, 512)
        t, _ = lax.optimization_barrier((t, after))
        return dot(t, up_weight).astype(bf16)

    up1 = up_of(1, tokens)
    up_c = along_z(up1, 1)
    up3 = up_of(3, up1)
    up_d = along_z(up3, -1)
    gate_out = gate_of(1 - xh, up3).astype(bf16)
    gate_in = across_x(gate_out)
    up2 = up_of(2, gate_out)
    up_a = two_along_z(up2)
    up_own = up_of(0, up2).astype(f32)
    gate_own = gate_of(xh, up2)

    gate = (gate_own + gate_in.astype(f32)).astype(bf16).reshape(8, 4, 8, UNITS + LANES)

    def gate_class(d):
        return pick(gate, (zl + d) & 3, 1).reshape(64, UNITS + LANES)

    gate_c = along_z(gate_class(1), 1)
    gate_d = along_z(gate_class(3), -1)
    gate_a = two_along_z(gate_class(2))
    up = (up_own + up_c.astype(f32) + up_d.astype(f32) + up_a.astype(f32)).reshape(2, 64, UNITS)
    up_in = across_x(pick(up, 1 - xh, 0).astype(bf16))
    up = pick(up, xh, 0) + up_in.astype(f32)
    gate = gate_class(0).astype(f32) + gate_c.astype(f32) + gate_d.astype(f32) + gate_a.astype(f32)

    both = jnp.concatenate([gate.astype(bf16), up.astype(bf16)], axis=1).reshape(4, 16, 2 * UNITS + LANES)
    far_a = along_z(pick(both, (zh + 1) & 3, 0), 4)
    far_b = along_z(pick(both, (zh + 3) & 3, 0), -4)
    far_c = along_z(pick(both, (zh + 2) & 3, 0), 8)

    rotated = pl.pallas_call(
        finish,
        out_shape=jax.ShapeDtypeStruct((16, UNITS), bf16),
        compiler_params=pltpu.CompilerParams(vmem_limit_bytes=4 * 1024 * 1024),
    )(pick(both, zh, 0), far_a, far_b, far_c, sign_bits.reshape(1, UNITS))

    far = lax.all_gather(rotated, "zh", axis=0, tiled=True)
    near = lax.all_gather(far, "xh", axis=0, tiled=True)
    n3 = along_z(near, 1)
    n1 = along_z(near, -1)
    n2 = jnp.concatenate([along_z(n1[:64], -1), along_z(n3[64:], 1)], axis=0)

    def out_of(group):
        pieces = [dot(v, down_weight).astype(bf16).reshape(16, 8, 512) for v in group]
        parts = lax.all_to_all(jnp.concatenate(pieces, axis=1), ("c", "y", "xl"), 0, 0, tiled=True)
        return jnp.sum(parts.astype(f32), axis=0).astype(bf16)

    out = jnp.concatenate([out_of(group) for group in ((near, n1, n2, n3),)], axis=0)
    out = jnp.concatenate([out, out], axis=0)
    return lax.dynamic_slice_in_dim(out, ((4 - zl) & 3) * 8, 32, 0)


def solution(mesh):
    fine = Mesh(mesh.devices.reshape(SIZES), AXES)
    return jax.shard_map(
        local,
        mesh=fine,
        in_specs=(P(GY, GX), P(GX, GY), P(GX, GY), P(GY, GX), P(GY)),
        out_specs=P(GY, GX),
        check_vma=False,
    )
```
